256 devices in a mesh: dp: 8 (over x, core), mp: 32 (over y, z).
Axes of the slice: x: 4, y: 4, z: 8, core: 2. Of those that a mesh axis runs over, the one named last changes fastest.
Arguments:
- tokens: bfloat16 [4096, 1024], P('dp'), may hold values from -52 to 52
- cotangent: bfloat16 [4096, 1024], P('dp'), may hold values from -12 to 12
- norm_gain: float32 [1024], replicated, may hold values from 0.5 to 1.5
- w_query: bfloat16 [1024, 16384], P(None, 'mp'), may hold values from -0.1875 to 0.1875
- w_key: bfloat16 [1024, 16384], P(None, 'mp'), may hold values from -0.1875 to 0.1875
- w_value: bfloat16 [1024, 16384], P(None, 'mp'), may hold values from -0.1875 to 0.1875
- w_out: bfloat16 [16384, 1024], P('mp'), may hold values from -0.046875 to 0.046875
- bias_table: float32 [128, 32], P('mp'), may hold values from -6 to 252
- buckets: int32 [1023], replicated, may hold values from 0 to 31, as said below
- qkv_rows: float32 [3, 1024], P(None, 'dp'), may hold values from 0.01 to 1
- qkv_cols: float32 [3, 16384], P(None, 'mp'), may hold values from 0.01 to 1
- out_rows: float32 [16384], P('mp'), may hold values from 3 to 300
- out_cols: float32 [1024], P('dp'), may hold values from 3 to 300
Outputs:
- grad_input: float32 [4096, 1024], P('dp')
- norm_gain_grad: float32 [1024], P('dp')
- bias_grad: float32 [128, 32], P('mp', 'dp')
- qkv_update: float32 [3, 1024, 16384], P(None, 'dp', 'mp')
- out_update: float32 [16384, 1024], P('mp', 'dp')
- qkv_rows_new: float32 [3, 1024], P(None, 'dp')
- qkv_cols_new: float32 [3, 16384], P(None, 'mp')
- out_rows_new: float32 [16384], P('mp')
- out_cols_new: float32 [1024], P('dp')
The draws below stay inside these ranges and needn't reach their ends.
Inputs may be any that keep to these rules, and one draw needn't show every extreme that they name: Entry j - i + 511 is the bucket of key position j seen from query position i of the same sequence. Keys after the query take the upper half of the buckets, the others the lower half; on each side the bucket never falls as the distance grows, distance 0 has bucket 0, and every distance of 128 or more takes that side's last bucket.
All inputs are finite; a program needn't handle non-finite values.
Results may differ from the reference program's by a relative error of at most 0.027.
Values may be sent and summed in bfloat16 or wider, within the bound.
A program may use at most 128 MiB of HBM per device.

```python
import math
import jax
import jax.numpy as jnp
from jax import lax

D = 1024
H = 128
DH = 128
NB = 32
MAXD = 128
LEN = 512
SEQS = 1
TOKENS = 4096
HD = 16384
N_DP = 8


def draw_tokens(key, part):
    key = jax.random.fold_in(key, 11)
    first_key, second_key, third_key = jax.random.split(key, 3)
    pattern = jnp.clip(jax.random.normal(first_key, (TOKENS, D), jnp.float32), -5.0, 5.0)
    lowest = 0.3
    highest = 3.0
    row_scale = jnp.exp(jax.random.uniform(second_key, (TOKENS, 1), jnp.float32, math.log(lowest), math.log(highest)))
    col_scale = jnp.exp(jax.random.uniform(third_key, (1, D), jnp.float32, math.log(lowest), math.log(highest)))
    return (pattern * row_scale * col_scale).astype(jnp.bfloat16)


def draw_bias_table(key, part):
    key = jax.random.fold_in(key, 12)
    first_key = jax.random.fold_in(key, 0)
    spread_noise = 1.5 * jnp.clip(jax.random.normal(first_key, (H, NB), jnp.float32), -4.0, 4.0)
    return spread_noise


def cut_points(side_key, side_count):
    chosen = jax.random.permutation(side_key, MAXD - 1)[:side_count - 2].astype(jnp.int32) + 1
    return jnp.concatenate([jnp.sort(chosen), jnp.full((1,), MAXD, jnp.int32)])


def draw_buckets(key, part):
    key = jax.random.fold_in(key, 13)
    ahead_key, behind_key = jax.random.split(key)
    side_count = NB // 2
    offsets = jnp.arange(2 * LEN - 1, dtype=jnp.int32) - (LEN - 1)
    distance = jnp.abs(offsets)
    ahead_cuts = cut_points(ahead_key, side_count)
    behind_cuts = cut_points(behind_key, side_count)
    count_ahead = jnp.sum((distance[:, None] >= ahead_cuts[None, :]).astype(jnp.int32), 1)
    count_behind = jnp.sum((distance[:, None] >= behind_cuts[None, :]).astype(jnp.int32), 1)
    bucket = jnp.where(offsets > 0, side_count + count_ahead, count_behind)
    return bucket.astype(jnp.int32)


def ramp_levels(key, leading, count, spread):
    levels = jnp.exp(jax.random.uniform(key, (leading, count), jnp.float32, math.log(0.1), 0.0))
    position = jnp.arange(count, dtype=jnp.float32) / count
    return levels * jnp.exp(-math.log(spread) * position)[None, :]


def draw_qkv_rows(key, part):
    key = jax.random.fold_in(key, 14)
    return ramp_levels(key, 3, D, 3.0)


def draw_qkv_cols(key, part):
    key = jax.random.fold_in(key, 15)
    return ramp_levels(key, 3, HD, 3.0)


def draw_out_rows(key, part):
    key = jax.random.fold_in(key, 16)
    return 300.0 * ramp_levels(key, 1, HD, 3.0)[0]


def draw_out_cols(key, part):
    key = jax.random.fold_in(key, 17)
    return 300.0 * ramp_levels(key, 1, D, 3.0)[0]


def strengthened(array, own_key, source, target, blocks, factor):
    owner, partner = [(jnp.arange(array.shape[dim]) // (array.shape[dim] // blocks)).reshape([-1 if axis == dim else 1 for axis in range(array.ndim)]) for dim in (source, target)]
    chosen = jax.random.permutation(own_key, blocks)[partner]
    strong = (owner == chosen) | (owner == (partner + blocks // 2) % blocks)
    return jnp.where(strong, factor * array, array)


def shard_levels(own_key, extent, cuts, low, largest):
    def one(dim, shards_of):
        heights = jax.random.uniform(jax.random.fold_in(jax.random.fold_in(own_key, 6), dim), (shards_of,), jnp.float32, low / len(cuts), largest / len(cuts))
        return jnp.repeat(jnp.exp(heights), extent[dim] // shards_of).reshape((-1,) + (1,) * (len(extent) - dim - 1))

    factor_of = one(*cuts[0])
    for cut in cuts[1:]:
        factor_of = factor_of * one(*cut)
    return factor_of


def bell_draw(own_key, shape, width, most, pieces=(), kind=jnp.bfloat16):
    array = jax.random.normal(own_key, shape, jnp.float32) * width
    if len(pieces) > 0:
        array = shard_levels(own_key, shape, pieces, -0.22, 0.18) * array
    return jnp.clip(array, min=-most, max=most).astype(kind)


def gaussian_with(rng, dims, scale, limit, shards, heavy, kind=jnp.bfloat16):
    entries = scale * jax.random.normal(rng, dims, jnp.float32)
    if shards:
        entries = entries * shard_levels(rng, dims, shards, -0.22, 0.18)
    return jnp.clip(strengthened(entries, jax.random.fold_in(rng, 3), *heavy), -limit, limit).astype(kind)


def setup_inputs(seed: int = 0) -> dict:
    seeds = jax.random.split(jax.random.key(seed), 14)
    tokens = draw_tokens(jax.random.fold_in(seeds[13], 71), 0)
    cotangent = gaussian_with(seeds[1], (TOKENS, D), 2.0, 12.0, ((0, 8),), (0, 1, 8, 2.0))
    norm_gain = jnp.clip(1.0 + 0.1 * jax.random.normal(seeds[2], (D,), jnp.float32), 0.5, 1.5)
    w_query = bell_draw(seeds[3], (D, HD), D ** -0.5, 0.1875, ((1, 32),))
    w_key = bell_draw(seeds[4], (D, HD), D ** -0.5, 0.1875, ((1, 32),))
    w_value = bell_draw(seeds[5], (D, HD), D ** -0.5, 0.1875, ((1, 32),))
    w_out = bell_draw(seeds[6], (HD, D), HD ** -0.5, 0.046875, ((0, 32),))
    bias_table = draw_bias_table(jax.random.fold_in(seeds[13], 71), 0)
    buckets = draw_buckets(jax.random.fold_in(seeds[13], 71), 0)
    qkv_rows = draw_qkv_rows(jax.random.fold_in(seeds[13], 71), 0)
    qkv_cols = draw_qkv_cols(jax.random.fold_in(seeds[13], 71), 0)
    out_rows = draw_out_rows(jax.random.fold_in(seeds[13], 71), 0)
    out_cols = draw_out_cols(jax.random.fold_in(seeds[13], 71), 0)
    return {"tokens": tokens, "cotangent": cotangent, "norm_gain": norm_gain, "w_query": w_query, "w_key": w_key, "w_value": w_value, "w_out": w_out, "bias_table": bias_table, "buckets": buckets, "qkv_rows": qkv_rows, "qkv_cols": qkv_cols, "out_rows": out_rows, "out_cols": out_cols}


decay_rate = 1.0 - 100.0 ** (-0.8)

def norm_backward(d_normed, normal, inverse, norm_gain):
    scaled = d_normed * norm_gain
    centre = lax.optimization_barrier(jnp.mean(scaled * normal, -1, keepdims=True))
    return ((scaled - normal * centre) * inverse, lax.optimization_barrier(jnp.sum(d_normed * normal, 0)))

def factored_step(gradient, rows_old, cols_old):
    squared = gradient * gradient
    rows_new = decay_rate * rows_old + (1.0 - decay_rate) * lax.optimization_barrier(jnp.mean(squared, 1))
    cols_new = decay_rate * cols_old + (1.0 - decay_rate) * lax.optimization_barrier(jnp.mean(squared, 0))
    raw_step = gradient * lax.rsqrt(rows_new[:, None] * cols_new[None, :])
    update = raw_step * lax.rsqrt(jnp.mean(raw_step * raw_step) + 1e-06)
    return (update, rows_new, cols_new)

def reference(tokens, cotangent, norm_gain, w_query, w_key, w_value, w_out, bias_table, buckets, qkv_rows, qkv_cols, out_rows, out_cols):
    scale_factor = DH ** (-0.5)
    positions = jnp.arange(LEN, dtype=jnp.int32)
    bucket_grid = buckets[positions[None, :] - positions[:, None] + (LEN - 1)]
    group_rows = SEQS * LEN

    def head_pass(inputs):
        query_head, key_head, value_head, d_att_head, table_row = inputs
        query_f = query_head.astype(jnp.float32)
        key_f = key_head.astype(jnp.float32)
        value_f = value_head.astype(jnp.float32)
        d_att_f = d_att_head.astype(jnp.float32)
        bias_tile = table_row[bucket_grid]
        scores = jnp.einsum('sqd,skd->sqk', query_f, key_f) * scale_factor + bias_tile[None]
        row_peak = lax.optimization_barrier(jnp.max(scores, -1, keepdims=True))
        weights = jnp.exp(scores - row_peak)
        attention = weights / lax.optimization_barrier(jnp.sum(weights, -1, keepdims=True))
        attention_low = lax.optimization_barrier(attention.astype(jnp.bfloat16)).astype(jnp.float32)
        attended = jnp.einsum('sqk,skd->sqd', attention_low, value_f).astype(jnp.bfloat16)
        d_value = jnp.einsum('sqk,sqd->skd', attention_low, d_att_f).astype(jnp.bfloat16)
        d_probs = jnp.einsum('sqd,skd->sqk', d_att_f, value_f)
        d_scores = attention * (d_probs - lax.optimization_barrier(jnp.sum(attention * d_probs, -1, keepdims=True)))
        d_low = lax.optimization_barrier(d_scores.astype(jnp.bfloat16)).astype(jnp.float32)
        d_query = (jnp.einsum('sqk,skd->sqd', d_low, key_f) * scale_factor).astype(jnp.bfloat16)
        d_key = (jnp.einsum('sqk,sqd->skd', d_low, query_f) * scale_factor).astype(jnp.bfloat16)
        bias_part = jax.ops.segment_sum(lax.optimization_barrier(jnp.sum(d_scores, 0)).reshape(-1), bucket_grid.reshape(-1), num_segments=NB)
        return (attended, d_value, d_query, d_key, bias_part)

    def to_heads(matrix):
        return matrix.reshape(SEQS, LEN, H, DH).transpose(2, 0, 1, 3)

    def from_heads(stacked):
        return stacked.transpose(1, 2, 0, 3).reshape(group_rows, HD)
    totals = [jnp.zeros((D, HD), jnp.float32), jnp.zeros((D, HD), jnp.float32), jnp.zeros((D, HD), jnp.float32), jnp.zeros((HD, D), jnp.float32), jnp.zeros((D,), jnp.float32), jnp.zeros((H, NB), jnp.float32)]
    grad_inputs = []
    for group_index in range(N_DP):
        group_tokens = tokens[group_index * group_rows:(group_index + 1) * group_rows]
        group_cot = cotangent[group_index * group_rows:(group_index + 1) * group_rows]
        float_tokens = group_tokens.astype(jnp.float32)
        inverse = lax.rsqrt(lax.optimization_barrier(jnp.mean(float_tokens * float_tokens, -1, keepdims=True)) + 1e-06)
        normal = float_tokens * inverse
        normed = (normal * norm_gain).astype(jnp.bfloat16)
        queries = jnp.dot(normed, w_query, preferred_element_type=jnp.float32).astype(jnp.bfloat16)
        key_rows = jnp.dot(normed, w_key, preferred_element_type=jnp.float32).astype(jnp.bfloat16)
        value_rows = jnp.dot(normed, w_value, preferred_element_type=jnp.float32).astype(jnp.bfloat16)
        d_attended = jnp.dot(group_cot, w_out.T, preferred_element_type=jnp.float32).astype(jnp.bfloat16)
        attended, d_value, d_query, d_key, bias_part = lax.map(head_pass, (to_heads(queries), to_heads(key_rows), to_heads(value_rows), to_heads(d_attended), bias_table))
        attended = from_heads(attended)
        d_value = from_heads(d_value)
        d_query = from_heads(d_query)
        d_key = from_heads(d_key)
        d_normed = jnp.dot(d_query, w_query.T, preferred_element_type=jnp.float32) + jnp.dot(d_key, w_key.T, preferred_element_type=jnp.float32) + jnp.dot(d_value, w_value.T, preferred_element_type=jnp.float32)
        group_grad, gain_part = norm_backward(d_normed, normal, inverse, norm_gain)
        grad_inputs.append(group_grad)
        parts = [jnp.dot(normed.T, d_query, preferred_element_type=jnp.float32), jnp.dot(normed.T, d_key, preferred_element_type=jnp.float32), jnp.dot(normed.T, d_value, preferred_element_type=jnp.float32), jnp.dot(attended.T, group_cot, preferred_element_type=jnp.float32), gain_part, bias_part]
        totals = [running + group_part.astype(jnp.bfloat16).astype(jnp.float32) for running, group_part in zip(totals, parts)]
    grad_input = jnp.concatenate(grad_inputs, 0)
    grad_query, grad_key, grad_value, grad_out, norm_gain_grad, bias_grad = totals
    query_update, query_rows, query_cols = factored_step(grad_query, qkv_rows[0], qkv_cols[0])
    key_update, key_rows_new, key_cols_new = factored_step(grad_key, qkv_rows[1], qkv_cols[1])
    value_update, value_rows_new, value_cols_new = factored_step(grad_value, qkv_rows[2], qkv_cols[2])
    out_update, out_rows_new, out_cols_new = factored_step(grad_out, out_rows, out_cols)
    qkv_update = jnp.stack([query_update, key_update, value_update])
    qkv_rows_new = jnp.stack([query_rows, key_rows_new, value_rows_new])
    qkv_cols_new = jnp.stack([query_cols, key_cols_new, value_cols_new])
    return (grad_input, norm_gain_grad, bias_grad, qkv_update, out_update, qkv_rows_new, qkv_cols_new, out_rows_new, out_cols_new)
```

```python
import functools

import jax
import jax.numpy as jnp
from jax import lax
from jax.experimental import pallas as pl
from jax.experimental.pallas import tpu as pltpu
from jax.sharding import PartitionSpec as P

D = 1024
DH = 128
NB = 32
LEN = 512
HD = 16384
HEADS = 4
N_DP = 8
N_Y = 4
N_Z = 8
SCALE = DH ** (-0.5)
DECAY = 1.0 - 100.0 ** (-0.8)
MESH = pl.DeviceIdType.MESH
BF = jnp.bfloat16
F32 = jnp.float32


def nn(a, b):
    return lax.dot_general(a, b, (((1,), (0,)), ((), ())), preferred_element_type=F32)


def nt(a, b):
    return lax.dot_general(a, b, (((1,), (1,)), ((), ())), preferred_element_type=F32)


def exact(a, b, contract):
    return lax.dot_general(
        a,
        b,
        ((contract[:1], contract[1:]), ((), ())),
        preferred_element_type=F32,
        precision=lax.Precision.HIGHEST,
    )


def kernel(
    tokens,
    cot,
    gain,
    w_query,
    w_key,
    w_value,
    w_out,
    table,
    reversed_buckets,
    qkv_rows,
    qkv_cols,
    out_rows,
    out_cols,
    grad_input,
    gain_grad,
    bias_grad,
    qkv_update,
    out_update,
    qkv_rows_new,
    qkv_cols_new,
    out_rows_new,
    out_cols_new,
    normed,
    normed_t,
    cot_t,
    normal,
    q_heads,
    k_heads,
    v_heads,
    da_heads,
    bias_rows,
    diagonals,
    att_low,
    ds_low,
    dq_all,
    dk_all,
    dv_all,
    onehot,
    grads,
    core_in,
    ring_a,
    ring_b,
    ring_l,
    ring_r,
    total,
    hidden,
    y_a,
    y_b,
    y_l,
    y_r,
    z_out,
    z_in,
    gathered,
    dp_box,
    y_box,
    z_box,
    last_box,
    core_send,
    core_recv,
    x_send,
    x_recv,
    y_send,
    y_recv,
    zs_send,
    zs_recv,
    zg_send,
    zg_recv,
    yg_send,
    yg_recv,
    dp_send,
    dp_recv,
    yb_send,
    yb_recv,
    zb_send,
    zb_recv,
    last_send,
    last_recv,
):
    dp = lax.axis_index("dp")
    mp = lax.axis_index("mp")
    core = lax.rem(dp, 2)
    x = lax.div(dp, 2)
    y = lax.div(mp, N_Z)
    z = lax.rem(mp, N_Z)

    def at_x(k):
        return lax.rem(x + k, 4)

    def at_y(k):
        return lax.rem(y + k, 4)

    def at_z(k):
        return lax.rem(z + k, N_Z)

    def dp_peer(k):
        return {"dp": lax.rem(dp + k, N_DP)}

    def x_peer(k):
        return {"dp": at_x(k) * 2 + core}

    def y_peer(k):
        return {"mp": at_y(k) * N_Z + z}

    def z_peer(k):
        return {"mp": y * N_Z + at_z(k)}

    barrier = pltpu.get_barrier_semaphore()
    for k in range(1, N_DP):
        pl.semaphore_signal(barrier, inc=1, device_id=dp_peer(k), device_id_type=MESH)
    for k in range(1, 4):
        pl.semaphore_signal(barrier, inc=1, device_id=y_peer(k), device_id_type=MESH)
    for k in range(1, N_Z):
        pl.semaphore_signal(barrier, inc=1, device_id=z_peer(k), device_id_type=MESH)

    def remote(src, dst, send, recv, peer):
        return pltpu.make_async_remote_copy(
            src_ref=src, dst_ref=dst, send_sem=send, recv_sem=recv, device_id=peer, device_id_type=MESH
        )

    floats = tokens[...].astype(F32)
    inverse = lax.rsqrt(jnp.mean(floats * floats, -1, keepdims=True) + 1e-06)
    normal[...] = floats * inverse
    normed[...] = (normal[...] * gain[...]).astype(BF)
    normed_t[...] = normed[...].T
    cot_t[...] = cot[...].T
    onehot[...] = (
        reversed_buckets[...] == lax.broadcasted_iota(jnp.int32, (NB, 1024), 0)
    ).astype(F32)
    per_offset = exact(table[...], onehot[...], (1, 0))
    for h in range(HEADS):
        wide = jnp.broadcast_to(per_offset[h : h + 1, :], (128, 1024))
        bias_rows[h] = pltpu.roll(wide, 897, 1, stride=1, stride_axis=0)
    for matrix, heads in ((w_query, q_heads), (w_key, k_heads), (w_value, v_heads)):
        product = nn(normed[...], matrix[...]).astype(BF)
        for h in range(HEADS):
            heads[h] = product[:, h * DH : (h + 1) * DH]
    product = nt(cot[...], w_out[...]).astype(BF)
    for h in range(HEADS):
        da_heads[h] = product[:, h * DH : (h + 1) * DH]

    def attend(h):
        query, key, value, d_att = q_heads[h], k_heads[h], v_heads[h], da_heads[h]
        started = set()
        for i in range(4):
            cols = slice(i * 128, (i + 1) * 128)
            scores = nt(key, query[cols, :]) * SCALE
            scores = scores + jnp.concatenate(
                [bias_rows[h, :, (i - b + 3) * 128 : (i - b + 4) * 128] for b in range(4)], 0
            )
            weights = jnp.exp(scores - jnp.max(scores, 0, keepdims=True))
            attention = weights * (1.0 / jnp.sum(weights, 0, keepdims=True))
            att_low[:, cols] = attention.astype(BF)
            d_probs = nt(value, d_att[cols, :])
            d_scores = attention * (d_probs - jnp.sum(attention * d_probs, 0, keepdims=True))
            ds_low[:, cols] = d_scores.astype(BF)
            for b in range(4):
                t = i - b + 3
                lanes = slice(t * 128, (t + 1) * 128)
                tile = d_scores[b * 128 : (b + 1) * 128, :]
                if t in started:
                    diagonals[h, :, lanes] = diagonals[h, :, lanes] + tile
                else:
                    diagonals[h, :, lanes] = tile
                    started.add(t)
        diagonals[h, :, 896:1024] = jnp.zeros((128, 128), F32)
        d_value = nn(att_low[...], d_att).astype(BF)
        d_key = (nn(ds_low[...], query) * SCALE).astype(BF)
        attended = nn(value.T, att_low[...]).astype(BF).T
        d_query = (nn(key.T, ds_low[...]) * SCALE).astype(BF).T
        lanes = pl.ds(pl.multiple_of(h * DH, DH), DH)
        dq_all[:, lanes] = d_query
        dk_all[:, lanes] = d_key
        dv_all[:, lanes] = d_value
        return attended, jnp.concatenate([d_query, d_key, d_value], 1)

    def weight_grads(h, attended, joined):
        for r in range(2):
            block = nn(normed_t[r * 512 : (r + 1) * 512, :], joined).astype(BF)
            last = nn(cot_t[r * 512 : (r + 1) * 512, :], attended).astype(BF)
            for s in range(4):
                p = r * 4 + s
                rows = slice(s * 128, (s + 1) * 128)
                for m in range(3):
                    grads[h, p % 2, p // 2, m * 128 : (m + 1) * 128, :] = block[
                        rows, m * 128 : (m + 1) * 128
                    ]
                grads[h, p % 2, p // 2, 384:512, :] = last[rows, :]

    top, low = slice(0, 256), slice(256, 512)

    def core_copy(h):
        return remote(
            grads.at[h, 1 - core], core_in.at[h], core_send.at[h], core_recv.at[h], {"dp": x * 2 + 1 - core}
        )

    def x_copy(h, n):
        src, dst, peer = (
            (grads.at[h, core, at_x(2), top], ring_a.at[h], 1),
            (grads.at[h, core, at_x(2), low], ring_b.at[h], 3),
            (grads.at[h, core, at_x(1), low], ring_r.at[h, low], 1),
            (grads.at[h, core, at_x(3), top], ring_l.at[h, top], 3),
            (grads.at[h, core, at_x(1), top], ring_r.at[h, top], 1),
            (grads.at[h, core, at_x(3), low], ring_l.at[h, low], 3),
        )[n]
        return remote(src, dst, x_send.at[h, n], x_recv.at[h, n], x_peer(peer))

    def add_into(ref, index, other):
        ref[index] = (ref[index].astype(F32) + other.astype(F32)).astype(BF)

    def x_first(h):
        core_copy(h).wait_recv()
        for k in (2, 1, 3, 0):
            add_into(grads, (h, core, at_x(k)), core_in[h, at_x(k)])
            if k == 2:
                x_copy(h, 0).start()
                x_copy(h, 1).start()
            elif k == 1:
                x_copy(h, 2).start()
            elif k == 3:
                x_copy(h, 3).start()

    def x_second(h):
        x_copy(h, 0).wait_recv()
        add_into(grads, (h, core, at_x(1), top), ring_a[h])
        x_copy(h, 4).start()
        x_copy(h, 1).wait_recv()
        add_into(grads, (h, core, at_x(3), low), ring_b[h])
        x_copy(h, 5).start()

    def x_third(h):
        for n in range(2, 6):
            x_copy(h, n).wait_recv()
        whole = grads[h, core, x].astype(F32) + ring_r[h].astype(F32) + ring_l[h].astype(F32)
        lanes = pl.ds(pl.multiple_of(h * DH, DH), DH)
        for m in range(4):
            total[m, :, lanes] = whole[m * 128 : (m + 1) * 128, :]

    pl.semaphore_wait(barrier, (N_DP - 1) + 3 + (N_Z - 1))

    def per_head(h, carry):
        attended, joined = attend(h)

        @pl.when(h >= 1)
        def _():
            x_first(h - 1)

        weight_grads(h, attended, joined)
        core_copy(h).start()

        @pl.when(h >= 1)
        def _():
            x_second(h - 1)

        @pl.when(h >= 2)
        def _():
            x_third(h - 2)

        return carry

    lax.fori_loop(0, HEADS, per_head, 0)

    gain_parts = []
    for c in range(4):
        cols = slice(c * 256, (c + 1) * 256)
        piece = (
            nt(dq_all[...], w_query[cols, :])
            + nt(dk_all[...], w_key[cols, :])
            + nt(dv_all[...], w_value[cols, :])
        )
        gain_parts.append(jnp.sum(piece * normal[:, cols], 0, keepdims=True))
        hidden[:, :, cols] = piece.astype(BF).reshape(4, 128, 256)

    y_top, y_low = slice(0, 64), slice(64, 128)

    def y_copy(n):
        src, dst, peer = (
            (hidden.at[at_y(2), y_top], y_a, 1),
            (hidden.at[at_y(2), y_low], y_b, 3),
            (hidden.at[at_y(1), y_low], y_r.at[y_low], 1),
            (hidden.at[at_y(3), y_top], y_l.at[y_top], 3),
            (hidden.at[at_y(1), y_top], y_r.at[y_top], 1),
            (hidden.at[at_y(3), y_low], y_l.at[y_low], 3),
        )[n]
        return remote(src, dst, y_send.at[n], y_recv.at[n], y_peer(peer))

    for n in range(4):
        y_copy(n).start()
    x_first(HEADS - 1)
    x_third(HEADS - 2)

    folded = diagonals[...]
    rows = 64
    while rows >= 8:
        folded = folded[:, :rows, :] + pltpu.roll(
            folded[:, rows:, :].reshape(HEADS * rows, 1024), 1024 - rows, 1
        ).reshape(HEADS, rows, 1024)
        rows //= 2
    sums = []
    for h in range(HEADS):
        line = folded[h, 0:1, :]
        for r in range(1, 8):
            line = line + pltpu.roll(folded[h, r : r + 1, :], 1024 - r, 1)
        sums.append(pltpu.roll(line, 127, 1))
    bias_part = exact(jnp.concatenate(sums, 0), onehot[...], (1, 1))

    y_copy(0).wait_recv()
    add_into(hidden, (at_y(1), y_top), y_a[...])
    y_copy(4).start()
    y_copy(1).wait_recv()
    add_into(hidden, (at_y(3), y_low), y_b[...])
    y_copy(5).start()
    x_second(HEADS - 1)

    def zs_copy(k):
        return remote(z_out.at[at_z(k)], z_in.at[k - 1], zs_send.at[k - 1], zs_recv.at[k - 1], z_peer(k))

    for n in range(2, 6):
        y_copy(n).wait_recv()
    z_out[...] = (
        (hidden[y].astype(F32) + y_r[...].astype(F32) + y_l[...].astype(F32))
        .astype(BF)
        .reshape(N_Z, 16, D)
    )
    for k in (4, 3, 5, 2, 6, 1, 7):
        zs_copy(k).start()

    x_third(HEADS - 1)
    dp_box[dp, 0:4, :] = jnp.concatenate(
        [jnp.sum(total[m] * total[m], 0, keepdims=True) for m in range(4)], 0
    )
    dp_box[dp, 4:5, :] = jnp.concatenate(gain_parts[:2], 1)
    dp_box[dp, 5:6, :] = jnp.concatenate(gain_parts[2:], 1)
    dp_box[dp, 6:8, :] = jnp.zeros((2, 512), F32)
    dp_box[dp, 8:16, :] = jnp.zeros((8, 512), F32)
    dp_box[dp, 8:12, 0:NB] = bias_part

    def dp_copy(k):
        return remote(dp_box.at[dp], dp_box.at[dp], dp_send.at[k - 1], dp_recv.at[k - 1], dp_peer(k))

    def dp_arrival(k):
        source = lax.rem(dp + N_DP - k, N_DP)
        return remote(dp_box.at[source], dp_box.at[source], dp_send.at[k - 1], dp_recv.at[k - 1], dp_peer(k))

    for k in range(1, N_DP):
        dp_copy(k).start()

    for k in range(1, N_Z):
        zs_copy(k).wait_recv()
    d_normed = z_out[z].astype(F32)
    for k in range(1, N_Z):
        d_normed = d_normed + z_in[k - 1].astype(F32)
    own = pl.ds(pl.multiple_of(mp * 16, 16), 16)
    own_floats = tokens[own, :].astype(F32)
    own_inverse = lax.rsqrt(jnp.mean(own_floats * own_floats, -1, keepdims=True) + 1e-06)
    own_normal = own_floats * own_inverse
    scaled = d_normed * gain[...]
    centre = jnp.mean(scaled * own_normal, -1, keepdims=True)
    gathered[y, z] = ((scaled - own_normal * centre) * own_inverse).astype(BF)

    def zg_copy(k):
        return remote(gathered.at[y, z], gathered.at[y, z], zg_send.at[k - 1], zg_recv.at[k - 1], z_peer(k))

    def zg_arrival(k):
        source = at_z(N_Z - k)
        return remote(gathered.at[y, source], gathered.at[y, source], zg_send.at[k - 1], zg_recv.at[k - 1], z_peer(k))

    for k in (4, 3, 5, 2, 6, 1, 7):
        zg_copy(k).start()

    for k in range(1, N_DP):
        dp_arrival(k).wait_recv()
    summed = dp_box[0]
    for s in range(1, N_DP):
        summed = summed + dp_box[s]
    bias_grad[...] = summed[8:12, 0:128]
    cols_old = jnp.concatenate([qkv_cols[...], out_rows[...]], 0)
    cols_new = DECAY * cols_old + (1.0 - DECAY) * (summed[0:4, :] / D)
    qkv_cols_new[...] = cols_new[0:3, :]
    out_rows_new[...] = cols_new[3:4, :]
    half = pl.ds(pl.multiple_of(lax.rem(dp, 4) * 128, 128), 128)
    line = lax.div(dp, 4)
    own_gain = jnp.zeros((1, 128), F32)
    for s in range(N_DP):
        pair = dp_box[s, 4:6, half]
        own_gain = own_gain + jnp.where(line == 0, pair[0:1, :], pair[1:2, :])
    lane = lax.broadcasted_iota(jnp.int32, (128, 128), 1)
    packed = jnp.zeros((128, 128), F32)
    for m in range(4):
        squared = total[m] * total[m]
        packed = jnp.where(lane == m, jnp.sum(squared, 1, keepdims=True), packed)
        weighted = jnp.sum(squared / cols_new[m : m + 1, :], 1, keepdims=True)
        packed = jnp.where(lane == m + 4, weighted, packed)
    y_box[y, 0:8, :] = packed.T[0:8, :]
    y_box[y, 8:16, :] = jnp.broadcast_to(own_gain, (8, 128))

    def yb_copy(k):
        return remote(y_box.at[y], y_box.at[y], yb_send.at[k - 1], yb_recv.at[k - 1], y_peer(k))

    def yb_arrival(k):
        source = at_y(4 - k)
        return remote(y_box.at[source], y_box.at[source], yb_send.at[k - 1], yb_recv.at[k - 1], y_peer(k))

    for k in range(1, 4):
        yb_copy(k).start()

    def yg_copy(n):
        first, second = pl.ds(0, 4), pl.ds(4, 4)
        ref, peer = (
            (gathered.at[y], 1),
            (gathered.at[y], 3),
            (gathered.at[at_y(3), first], 1),
            (gathered.at[at_y(1), second], 3),
        )[n]
        return remote(ref, ref, yg_send.at[n], yg_recv.at[n], y_peer(peer))

    def yg_arrival(n):
        first, second = pl.ds(0, 4), pl.ds(4, 4)
        ref = (
            gathered.at[at_y(3)],
            gathered.at[at_y(1)],
            gathered.at[at_y(2), first],
            gathered.at[at_y(2), second],
        )[n]
        return remote(ref, ref, yg_send.at[n], yg_recv.at[n], y_peer(1))

    for k in range(1, N_Z):
        zg_arrival(k).wait_recv()
    yg_copy(0).start()
    yg_copy(1).start()

    for k in range(1, 4):
        yb_arrival(k).wait_recv()
    z_box[z] = y_box[0] + y_box[1] + y_box[2] + y_box[3]

    def zb_copy(k):
        return remote(z_box.at[z], z_box.at[z], zb_send.at[k - 1], zb_recv.at[k - 1], z_peer(k))

    def zb_arrival(k):
        source = at_z(N_Z - k)
        return remote(z_box.at[source], z_box.at[source], zb_send.at[k - 1], zb_recv.at[k - 1], z_peer(k))

    for k in range(1, N_Z):
        zb_copy(k).start()

    yg_arrival(0).wait_recv()
    yg_copy(2).start()
    yg_arrival(1).wait_recv()
    yg_copy(3).start()

    for k in range(1, N_Z):
        zb_arrival(k).wait_recv()
    row_sums = z_box[0]
    for s in range(1, N_Z):
        row_sums = row_sums + z_box[s]
    gain_grad[...] = row_sums[8:9, :]
    rows_old = jnp.concatenate([qkv_rows[...], out_cols[...]], 0)
    rows_new = DECAY * rows_old + (1.0 - DECAY) * (row_sums[0:4, :] / HD)
    qkv_rows_new[...] = rows_new[0:3, :]
    out_cols_new[...] = rows_new[3:4, :]
    ratio = row_sums[4:8, :] / rows_new
    last_box[dp] = jnp.concatenate([ratio, jnp.zeros((4, 128), F32)], 0)

    def last_copy(k):
        return remote(last_box.at[dp], last_box.at[dp], last_send.at[k - 1], last_recv.at[k - 1], dp_peer(k))

    def last_arrival(k):
        source = lax.rem(dp + N_DP - k, N_DP)
        return remote(last_box.at[source], last_box.at[source], last_send.at[k - 1], last_recv.at[k - 1], dp_peer(k))

    for k in range(1, N_DP):
        last_copy(k).start()

    for n in range(2, 4):
        yg_arrival(n).wait_recv()
    grad_input[...] = gathered[...].astype(F32).reshape(LEN, D)

    for k in range(1, N_DP):
        last_arrival(k).wait_recv()
    raw_total = last_box[0]
    for s in range(1, N_DP):
        raw_total = raw_total + last_box[s]
    mean_square = jnp.sum(raw_total, 1, keepdims=True) / float(D * HD)
    row_scale = jnp.concatenate(
        [lax.rsqrt(rows_new) * lax.rsqrt(mean_square[0:4, :] + 1e-06), jnp.zeros((124, 128), F32)], 0
    ).T
    for m in range(4):
        update = total[m] * row_scale[:, m : m + 1] * lax.rsqrt(cols_new[m : m + 1, :])
        if m < 3:
            qkv_update[m] = update
        else:
            out_update[...] = update.T

    def drain(h, carry):
        core_copy(h).wait_send()
        for n in range(6):
            x_copy(h, n).wait_send()
        return carry

    lax.fori_loop(0, HEADS, drain, 0)
    for n in range(6):
        y_copy(n).wait_send()
    for k in range(1, N_Z):
        zs_copy(k).wait_send()
        zg_copy(k).wait_send()
        zb_copy(k).wait_send()
    for n in range(4):
        yg_copy(n).wait_send()
    for k in range(1, 4):
        yb_copy(k).wait_send()
    for k in range(1, N_DP):
        dp_copy(k).wait_send()
        last_copy(k).wait_send()


def pairs(*shape):
    return [pltpu.SemaphoreType.DMA(shape)] * 2


def on_device(
    tokens,
    cotangent,
    norm_gain,
    w_query,
    w_key,
    w_value,
    w_out,
    bias_table,
    buckets,
    qkv_rows,
    qkv_cols,
    out_rows,
    out_cols,
):
    reversed_buckets = jnp.concatenate([buckets[::-1], jnp.full((1,), -1, jnp.int32)])[None]
    vmem = pl.BlockSpec(memory_space=pltpu.VMEM)
    outs = pl.pallas_call(
        kernel,
        out_shape=[
            jax.ShapeDtypeStruct((LEN, D), F32),
            jax.ShapeDtypeStruct((1, 128), F32),
            jax.ShapeDtypeStruct((HEADS, 128), F32),
            jax.ShapeDtypeStruct((3, 128, 512), F32),
            jax.ShapeDtypeStruct((512, 128), F32),
            jax.ShapeDtypeStruct((3, 128), F32),
            jax.ShapeDtypeStruct((3, 512), F32),
            jax.ShapeDtypeStruct((1, 512), F32),
            jax.ShapeDtypeStruct((1, 128), F32),
        ],
        in_specs=[vmem] * 13,
        out_specs=[vmem] * 9,
        scratch_shapes=[
            pltpu.VMEM((LEN, D), BF),
            pltpu.VMEM((D, LEN), BF),
            pltpu.VMEM((D, LEN), BF),
            pltpu.VMEM((LEN, D), F32),
            pltpu.VMEM((HEADS, LEN, DH), BF),
            pltpu.VMEM((HEADS, LEN, DH), BF),
            pltpu.VMEM((HEADS, LEN, DH), BF),
            pltpu.VMEM((HEADS, LEN, DH), BF),
            pltpu.VMEM((HEADS, 128, 1024), F32),
            pltpu.VMEM((HEADS, 128, 1024), F32),
            pltpu.VMEM((LEN, LEN), BF),
            pltpu.VMEM((LEN, LEN), BF),
            pltpu.VMEM((LEN, HEADS * DH), BF),
            pltpu.VMEM((LEN, HEADS * DH), BF),
            pltpu.VMEM((LEN, HEADS * DH), BF),
            pltpu.VMEM((NB, 1024), F32),
            pltpu.VMEM((HEADS, 2, 4, 512, DH), BF),
            pltpu.VMEM((HEADS, 4, 512, DH), BF),
            pltpu.VMEM((HEADS, 256, DH), BF),
            pltpu.VMEM((HEADS, 256, DH), BF),
            pltpu.VMEM((HEADS, 512, DH), BF),
            pltpu.VMEM((HEADS, 512, DH), BF),
            pltpu.VMEM((4, 128, 512), F32),
            pltpu.VMEM((4, 128, D), BF),
            pltpu.VMEM((64, D), BF),
            pltpu.VMEM((64, D), BF),
            pltpu.VMEM((128, D), BF),
            pltpu.VMEM((128, D), BF),
            pltpu.VMEM((N_Z, 16, D), BF),
            pltpu.VMEM((N_Z - 1, 16, D), BF),
            pltpu.VMEM((4, N_Z, 16, D), BF),
            pltpu.VMEM((N_DP, 16, 512), F32),
            pltpu.VMEM((4, 16, 128), F32),
            pltpu.VMEM((N_Z, 16, 128), F32),
            pltpu.VMEM((N_DP, 8, 128), F32),
            *pairs(HEADS),
            *pairs(HEADS, 6),
            *pairs(6),
            *pairs(N_Z - 1),
            *pairs(N_Z - 1),
            *pairs(4),
            *pairs(N_DP - 1),
            *pairs(3),
            *pairs(N_Z - 1),
            *pairs(N_DP - 1),
        ],
        compiler_params=pltpu.CompilerParams(
            collective_id=0, has_side_effects=True, vmem_limit_bytes=56 * 1024 * 1024
        ),
    )(
        tokens,
        cotangent,
        norm_gain[None],
        w_query,
        w_key,
        w_value,
        w_out,
        bias_table,
        reversed_buckets,
        qkv_rows,
        qkv_cols,
        out_rows[None],
        out_cols[None],
    )
    grad_input, gain, bias, qkv_update, out_update, rows_new, cols_new, orows_new, ocols_new = outs
    bias = lax.dynamic_slice_in_dim(bias[:, :NB], lax.axis_index("dp") * 4, 4, 1)
    return (
        grad_input,
        gain[0],
        bias,
        qkv_update,
        out_update,
        rows_new,
        cols_new,
        orows_new[0],
        ocols_new[0],
    )


def solution(mesh):
    return jax.shard_map(
        on_device,
        mesh=mesh,
        in_specs=(
            P("dp", None),
            P("dp", None),
            P(),
            P(None, "mp"),
            P(None, "mp"),
            P(None, "mp"),
            P("mp", None),
            P("mp", None),
            P(),
            P(None, "dp"),
            P(None, "mp"),
            P("mp"),
            P("dp"),
        ),
        out_specs=(
            P("dp", None),
            P("dp"),
            P("mp", "dp"),
            P(None, "dp", "mp"),
            P("mp", "dp"),
            P(None, "dp"),
            P(None, "mp"),
            P("mp"),
            P("dp"),
        ),
        check_vma=False,
    )
```
